128 devices in a mesh: gx: 32 (over z, x, core), gz: 4 (over y).
Axes of the slice: x: 4, y: 4, z: 4, core: 2. Of those that a mesh axis runs over, the one named last changes fastest.
Arguments:
- heads: bfloat16 [16, 4, 2048, 2048], P(None, 'gz', 'gx'), may hold values from -6 to 6
- leak: float32 [4, 2048, 2048], P('gz', 'gx'), may hold values from 0.05 to 0.3
- x_inverse: bfloat16 [4, 2048, 2048], P('gz')
- y_inverse: bfloat16 [4, 2048, 2048], P('gz')
- misfit: float32 [32768, 16], P(('gx', 'gz')), may hold values from -6 to 6
- row_owner: int32 [32768, 1], P(('gx', 'gz')), may hold values from 0 to 127; in each aligned block of 256 rows (0 to 255, 256 to 511, ...) at most 4 rows name the same one
- row_count: int32 [128], P(('gx', 'gz')), may hold values from 1 to 256, 16384 in all
- row_x: int32 [32768], P(('gx', 'gz')), may hold values from 0 to 63
- row_seg: int32 [32768], P(('gx', 'gz')), may hold values from 0 to 15
Outputs:
- adjoint: bfloat16 [16, 4, 2048, 2048], P(None, 'gz', 'gx')
- gradient: float32 [128, 16, 128], P(('gx', 'gz'))
The draws below stay inside these ranges and needn't reach their ends.
Inputs may be any that keep to these rules, and one draw needn't show every extreme that they name: `row_owner`: within the rows of one device (aligned blocks of 256 rows) no owner is named by more than 4 rows, a bound that some block reaches. Only the first row_count[d] rows of device d are live.
All inputs are finite; a program needn't handle non-finite values.
Results may differ from the reference program's by a relative error of at most 0.0057.
Values may be sent and summed in bfloat16 or wider, within the bound.
No kernel may reach another device: no remote copies, remote signals or barrier semaphores. Data moves between devices by JAX's collectives and lax.ppermute only.
A program may use at most 128 MiB of HBM per device.

```python
import math
import jax
import jax.numpy as jnp
import numpy as np
from jax import lax

NX = 2048
NY = 2048
SEG = 128
TESTS = 16
R_DEV = 256
NZ = 4
ROWS_TOTAL = 16384
CAP = 4
N_GX = 32
N_GZ = 4
DEVICES = 128


def line_inverse(key, cells):
    first, second = jax.random.split(key)
    diagonal = jax.random.uniform(first, (NZ, cells), jnp.float32, 0.5, 1.0)
    spread = jax.random.normal(second, (NZ, cells, cells), jnp.float32) * (0.5 / math.sqrt(cells))
    return spread + jnp.eye(cells, dtype=jnp.float32)[None] * diagonal[:, :, None]


def draw_x_inverse(key, part):
    return line_inverse(jax.random.fold_in(key, 11), NX).astype(jnp.bfloat16)


def draw_y_inverse(key, part):
    return line_inverse(jax.random.fold_in(key, 12), NY).astype(jnp.bfloat16)


def place_ends(result, stream_key, smallest, largest):
    extent = result.shape
    index_at = [jax.random.randint(jax.random.fold_in(stream_key, axis), (), 0, extent[axis]) for axis in range(len(extent))]
    result = result.at[tuple(index_at)].set(smallest)
    longest = extent.index(max(extent))
    index_at[longest] = (index_at[longest] + 1) % extent[longest]
    return result.at[tuple(index_at)].set(largest)


def block_scale(own_key, shape, cuts, low, largest):
    level, own = 1.0, jax.random.fold_in(own_key, 6)
    for position, shards_of in cuts:
        steps = jnp.exp(jax.random.uniform(jax.random.fold_in(own, position), (shards_of,), jnp.float32, low / len(cuts), largest / len(cuts)))
        level = level * jnp.repeat(steps, shape[position] // shards_of).reshape([-1 if axis == position else 1 for axis in range(len(shape))])
    return level


def profile(count, total, limit, lean):
    portions = [(1 << 20) // math.isqrt(grade ** lean) + 1 for grade in range(2, count + 1)]
    rest, given = total - limit - (count - 1), [1] * (count - 1)
    while rest > 0:
        candidates = [i for i in range(count - 1) if given[i] < limit]
        mass, left = sum([portions[i] for i in candidates]), rest
        for i in candidates:
            addition = min(limit - given[i], max(1, left * portions[i] // mass), rest)
            given[i] = given[i] + addition
            rest = rest - addition
    return np.array([limit] + given)


def ragged(own_key, amount, total, reach, slope):
    if amount == 2:
        one = jax.random.randint(own_key, (), max(1, total - reach), min(reach, total - 1) + 1)
        return jnp.stack([one, total - one])
    lengths = jnp.asarray(profile(amount, total, reach, slope), jnp.int32)
    couples = (amount - 1) // 2
    donor, sink = lengths[1:1 + 2 * couples:2], lengths[2:2 + 2 * couples:2]
    room = jnp.minimum(donor - 1, reach - sink)
    moved = jax.random.randint(jax.random.fold_in(own_key, 1), (couples,), 0, 1 << 20) % (room + 1)
    lengths = lengths.at[1:1 + 2 * couples:2].set(donor - moved).at[2:2 + 2 * couples:2].set(sink + moved)
    return lengths[jax.random.permutation(jax.random.fold_in(own_key, 2), amount)]


def routed_block(own_key, own, number, rows, amount, top, limit, skew):
    sequence = jax.random.permutation(own_key, amount)
    heavy_load, ordinary = shares(amount, rows * top, limit, skew, True), shares(amount, rows * top, limit, skew, False)
    places = jnp.arange(amount)

    def named(sizes, turn):
        used = int((sizes > 0).sum())
        fixed = max(1, used // 4)
        passed = fixed + (places - fixed + turn * (used - fixed)) % max(1, amount - fixed)
        return jnp.zeros((amount,), jnp.int32).at[sequence[jnp.where(places < fixed, places, passed)]].set(jnp.asarray(sizes, jnp.int32))

    sizes = jnp.where(number % 4 == 0, named(heavy_load, number // 4), named(ordinary, number - number // 4 - 1))
    mixed = jax.random.permutation(jax.random.fold_in(own, 3), amount)
    giver, sink = mixed[0:amount // 2 * 2:2], mixed[1:amount // 2 * 2:2]
    room = jnp.minimum(sizes[giver] - 1, limit - sizes[sink]) // 2
    room = jnp.where((giver == sequence[0]) | (sink == sequence[0]) | (sizes[sink] == 0), 0, jnp.maximum(room, 0))
    passed = jax.random.randint(jax.random.fold_in(own, 4), (amount // 2,), 0, 1 << 20) % (room + 1)
    sizes = sizes.at[giver].add(-passed).at[sink].add(passed)
    items = jnp.searchsorted(jnp.cumsum(sizes), jnp.arange(rows * top), side="right").astype(jnp.int32)
    listing = items.reshape(top, rows).T
    listing = listing[jax.random.permutation(jax.random.fold_in(own, 1), rows)]
    turn = jax.random.randint(jax.random.fold_in(own, 2), (rows, 1), 0, top)
    return jnp.take_along_axis(listing, (jnp.arange(top)[None, :] + turn) % top, axis=1)


def shares(number_of, total, limit, slope, full):
    portions = [(1 << 20) // math.isqrt(grade ** slope) + 1 for grade in range(1, number_of + 1)]
    largest = limit if full else min(limit, max(-(-total // number_of), total * portions[0] // sum(portions)))
    least = 1 if total - largest >= number_of - 1 else 0
    counts, surplus = [largest] + [least] * (number_of - 1), total - largest - least * (number_of - 1)
    while surplus > 0:
        candidates = [i for i in range(1, number_of) if counts[i] < largest] or [i for i in range(1, number_of) if counts[i] < limit]
        pool, budget = sum([portions[i] for i in candidates]), surplus
        for i in candidates:
            extra = min(limit - counts[i], max(1, budget * portions[i] // pool), surplus)
            counts[i] = counts[i] + extra
            surplus = surplus - extra
    return np.array(counts)


def normal_values(rng, shape, scale, reach, cuts=(), kind=jnp.bfloat16):
    result = jax.random.normal(rng, shape, jnp.float32) * scale
    if len(cuts) > 0:
        result = block_scale(rng, shape, cuts, -0.22, 0.18) * result
    return jnp.clip(result, min=-reach, max=reach).astype(kind)


def setup_inputs(seed: int = 0) -> dict:
    keys = jax.random.split(jax.random.key(seed), 10)
    heads = normal_values(keys[0], (TESTS, NZ, NY, NX), 1.0, 6.0, ((1, 4), (2, 32)))
    leak = jnp.clip(jnp.exp(math.log(0.3) - 1.7917595 * jax.random.uniform(keys[1], (NZ, NY, NX), jnp.float32) ** block_scale(keys[1], (NZ, NY, NX), ((0, 4), (1, 32)), -0.2, 0.2)), 0.05, 0.3)
    x_inverse = draw_x_inverse(jax.random.fold_in(keys[9], 71), 0)
    y_inverse = draw_y_inverse(jax.random.fold_in(keys[9], 71), 0)
    misfit = normal_values(keys[4], (DEVICES * R_DEV, TESTS), 1.0, 6.0, ((0, 128),), jnp.float32)
    row_owner_keys = jax.random.split(jax.random.fold_in(keys[5], 1), (DEVICES * R_DEV) // R_DEV)
    row_owner_turns = jax.random.permutation(jax.random.fold_in(keys[5], 3), (DEVICES * R_DEV) // R_DEV)
    row_owner = jax.vmap(lambda own, number: routed_block(jax.random.fold_in(keys[5], 2), own, number, R_DEV, DEVICES, 1, CAP, 2))(row_owner_keys, row_owner_turns).reshape((DEVICES * R_DEV, 1))
    row_count = ragged(keys[6], DEVICES, ROWS_TOTAL, R_DEV, 2).astype(jnp.int32)
    row_x = place_ends(jax.random.randint(keys[7], (DEVICES * R_DEV,), 0, NX // N_GX), jax.random.fold_in(keys[7], 1), 0, (NX // N_GX) - 1).astype(jnp.int32)
    row_seg = place_ends(jax.random.randint(keys[8], (DEVICES * R_DEV,), 0, NY // SEG), jax.random.fold_in(keys[8], 1), 0, (NY // SEG) - 1).astype(jnp.int32)
    return {"heads": heads, "leak": leak, "x_inverse": x_inverse, "y_inverse": y_inverse, "misfit": misfit, "row_owner": row_owner, "row_count": row_count, "row_x": row_x, "row_seg": row_seg}


def reference(heads, leak, x_inverse, y_inverse, misfit, row_owner, row_count, row_x, row_seg):
    centre = heads.astype(jnp.float32)
    padded = jnp.pad(centre, ((0, 0), (1, 1), (0, 0), (0, 0)))
    vertical = (centre + leak[None] * (padded[:, 2:] + padded[:, :-2] - 2.0 * centre)).astype(jnp.bfloat16)
    layers = []
    for layer_index in range(NZ):
        flat_rows = vertical[:, layer_index].reshape(TESTS * NY, NX)
        x_swept = lax.dot_general(flat_rows, x_inverse[layer_index], (((1,), (1,)), ((), ())),
                                  preferred_element_type=jnp.float32).astype(jnp.bfloat16)
        x_swept = x_swept.reshape(TESTS, NY, NX)
        y_swept = jnp.einsum('tjx,ij->txi', x_swept.astype(jnp.float32), y_inverse[layer_index].astype(jnp.float32),
                             precision=lax.Precision.HIGHEST).astype(jnp.bfloat16)
        layers.append(y_swept)
    adjoint = jnp.stack(layers, axis=1)
    device_total = N_GX * N_GZ
    x_local = NX // N_GX
    segments = NY // SEG
    global_row = jnp.arange(device_total * R_DEV, dtype=jnp.int32)
    device_row = global_row // R_DEV
    gx_index = device_row // N_GZ
    gz_index = device_row % N_GZ
    x_cell = gx_index * x_local + row_x
    live_rows = ((global_row % R_DEV) < row_count[device_row]).astype(jnp.float32)
    blocks = adjoint.reshape(TESTS, NZ, NX, segments, SEG)
    picked = blocks[:, gz_index, x_cell, row_seg, :].astype(jnp.float32)
    weighted = picked * (jnp.transpose(misfit) * live_rows[None, :])[:, :, None]
    gradient = jax.ops.segment_sum(jnp.transpose(weighted, (1, 0, 2)), row_owner[:, 0], num_segments=device_total)
    return adjoint, gradient
```

```python
import functools

import jax
import jax.numpy as jnp
from jax import lax
from jax.experimental import pallas as pl
from jax.experimental.pallas import tpu as pltpu
from jax.sharding import PartitionSpec as P

SEG = 128
CHUNKS = (2, 2, 2, 2)
BLOCK = 512
LIMIT = 52
NT = (((1,), (1,)), ((), ()))
MIB = 1 << 20
ANY = pl.BlockSpec(memory_space=pl.ANY)
VMEM = pl.BlockSpec(memory_space=pltpu.VMEM)
SMEM = pl.BlockSpec(memory_space=pltpu.SMEM)


def params(mib):
    return pltpu.CompilerParams(vmem_limit_bytes=mib * MIB)


def cost(flops, nbytes):
    return pl.CostEstimate(flops=flops, bytes_accessed=nbytes, transcendentals=0)


def fetch(source, buffer, sem):
    copy = pltpu.make_async_copy(source, buffer, sem)
    copy.start()
    return copy


def split_kernel(first, heads, out, sem):
    fetch(heads.at[pl.ds(first, out.shape[0])], out, sem).wait()


def split(heads, first, size):
    return pl.pallas_call(
        functools.partial(split_kernel, first),
        in_specs=[ANY],
        out_specs=ANY,
        out_shape=jax.ShapeDtypeStruct((size,) + heads.shape[1:], heads.dtype),
        scratch_shapes=[pltpu.SemaphoreType.DMA],
        compiler_params=params(LIMIT),
        cost_estimate=cost(0, 2 * MIB),
        name="split",
    )(heads)


def prepare_kernel(gz_count, x_local, count, misfit, owner, cells, hot, *weights):
    rows = owner.shape[1]
    lanes = lax.broadcasted_iota(jnp.int32, hot.shape, 1)
    hot[...] = (cells[...] == lanes).astype(jnp.float32).astype(jnp.bfloat16)

    m = weights[0].shape[1] // 2
    line = lax.broadcasted_iota(jnp.int32, (m, 2 * rows), 0)
    lane = lax.broadcasted_iota(jnp.int32, (m, 2 * rows), 1)
    test = (line // gz_count) % 2
    device = (line // (2 * gz_count)) * gz_count + line % gz_count
    owners = jnp.concatenate([owner[...], owner[...]], axis=1)
    keep = (owners == device) & (lane // rows == test) & (lane % rows < count[0])
    pair = 0
    for out in weights:
        for p in range(out.shape[0]):
            full = jnp.where(keep, misfit[pair : pair + 1], 0.0)
            high = full.astype(jnp.bfloat16)
            out[p, :m] = high
            out[p, m:] = (full - high.astype(jnp.float32)).astype(jnp.bfloat16)
            pair += 1


def prepare(misfit, row_owner, row_count, row_x, row_seg, x_local, segments, gx_count, gz_count):
    rows, tests = misfit.shape
    m = 2 * gx_count * gz_count
    cell = (row_seg * x_local + row_x).reshape(rows, 1)
    return pl.pallas_call(
        functools.partial(prepare_kernel, gz_count, x_local),
        in_specs=[SMEM, VMEM, VMEM, VMEM],
        out_specs=[VMEM] * (1 + len(CHUNKS)),
        out_shape=[jax.ShapeDtypeStruct((rows, x_local * segments), jnp.bfloat16)]
        + [jax.ShapeDtypeStruct((size, 2 * m, 2 * rows), jnp.bfloat16) for size in CHUNKS],
        compiler_params=params(40),
        cost_estimate=cost(0, 6 * MIB),
        name="prepare",
    )(row_count, misfit.T.reshape(tests // 2, 2 * rows), row_owner.T, cell)


def x_kernel(
    first, own, above, below, leak, inverse, after, out,
    own_v, above_v, below_v, leak_v, inverse_v, vertical, staged, sems, block_sems, out_sems,
):
    tests, _, lines, _ = own_v.shape
    inputs = [
        fetch(source, buffer, sems.at[i])
        for i, (source, buffer) in enumerate(
            [
                (leak, leak_v),
                (own.at[pl.ds(first, tests)], own_v),
                (above, above_v),
                (below, below_v),
            ]
        )
    ]
    cells = staged.shape[0]
    blocks = [
        fetch(
            inverse.at[:, pl.ds(k, BLOCK)], inverse_v.at[:, pl.ds(k, BLOCK)], block_sems.at[k // BLOCK]
        )
        for k in range(0, cells, BLOCK)
    ]
    for copy in inputs:
        copy.wait()
    for t in range(tests):
        centre = own_v[t, 0].astype(jnp.float32)
        near = above_v[t, 0].astype(jnp.float32) + below_v[t, 0].astype(jnp.float32)
        vertical[t * lines : (t + 1) * lines] = (
            centre + leak_v[0] * (near - 2.0 * centre)
        ).astype(jnp.bfloat16)
    sent = []
    for k in range(0, cells, BLOCK):
        blocks[k // BLOCK].wait()
        swept = lax.dot_general(
            vertical[...], inverse_v[0, k : k + BLOCK], NT, preferred_element_type=jnp.float32
        ).astype(jnp.bfloat16)
        staged[k : k + BLOCK] = swept.T
        sent.append(
            fetch(staged.at[pl.ds(k, BLOCK)], out.at[pl.ds(k, BLOCK)], out_sems.at[k // BLOCK])
        )
    for copy in sent:
        copy.wait()


def x_sweep(own, first, above, below, leak, inverse, after):
    tests, _, lines, width = above.shape
    cells = inverse.shape[1]
    part = pltpu.VMEM(above.shape, above.dtype)
    return pl.pallas_call(
        functools.partial(x_kernel, first),
        in_specs=[ANY] * 6,
        out_specs=ANY,
        out_shape=jax.ShapeDtypeStruct((cells, tests * lines), jnp.bfloat16),
        scratch_shapes=[
            part,
            part,
            part,
            pltpu.VMEM(leak.shape, leak.dtype),
            pltpu.VMEM(inverse.shape, inverse.dtype),
            pltpu.VMEM((tests * lines, width), jnp.bfloat16),
            pltpu.VMEM((cells, tests * lines), jnp.bfloat16),
            pltpu.SemaphoreType.DMA((4,)),
            pltpu.SemaphoreType.DMA((cells // BLOCK,)),
            pltpu.SemaphoreType.DMA((cells // BLOCK,)),
        ],
        compiler_params=params(LIMIT),
        cost_estimate=cost(2 * cells * tests * lines * width, 20 * MIB),
        name="x_sweep",
    )(own, above, below, leak, inverse, after)


def y_kernel(first, earlier, swept, inverse, hot, weights, *rest):
    befores = rest[:earlier]
    out, partial, swept_v, inverse_v, hot_v, weights_v, lines, staged, picked, sems, block_sems, out_sems = rest[-12:]
    inputs = [
        fetch(source, buffer, sems.at[i])
        for i, (source, buffer) in enumerate(
            [(swept, swept_v), (hot, hot_v), (weights, weights_v)]
        )
    ]
    sources, x_local, lanes = swept_v.shape
    pairs = lanes // SEG
    tests = 2 * pairs
    y_local = SEG // 2
    cells = inverse_v.shape[1]
    blocks = [
        fetch(
            inverse.at[:, pl.ds(k, BLOCK)], inverse_v.at[:, pl.ds(k, BLOCK)], block_sems.at[k // BLOCK]
        )
        for k in range(0, cells, BLOCK)
    ]

    group = weights_v.shape[1] // 2 // sources
    place = 0
    for before in befores:
        partial[:, place : place + before.shape[1]] = before[...]
        place += before.shape[1]

    inputs[0].wait()
    for p in range(pairs):
        for s in range(sources // 2):
            a = swept_v[2 * s, :, p * SEG : (p + 1) * SEG]
            b = swept_v[2 * s + 1, :, p * SEG : (p + 1) * SEG]
            for t in range(2):
                cut = slice(t * y_local, (t + 1) * y_local)
                lines[
                    (2 * p + t) * x_local : (2 * p + t + 1) * x_local,
                    s * SEG : (s + 1) * SEG,
                ] = jnp.concatenate([a[:, cut], b[:, cut]], axis=1)

    sent = []
    for k in range(0, cells, BLOCK):
        blocks[k // BLOCK].wait()
        done = lax.dot_general(
            lines[...], inverse_v[0, k : k + BLOCK], NT, preferred_element_type=jnp.float32
        ).astype(jnp.bfloat16)
        for t in range(tests):
            staged[t, 0, :, k : k + BLOCK] = done[t * x_local : (t + 1) * x_local]
        sent.append(
            fetch(
                staged.at[:, :, :, pl.ds(k, BLOCK)],
                out.at[pl.ds(first, tests), :, :, pl.ds(k, BLOCK)],
                out_sems.at[k // BLOCK],
            )
        )
        if k == 0:
            inputs[1].wait()
        first_cell = k // SEG * x_local
        for p in range(pairs):
            stack = []
            for s in range(0, BLOCK, SEG):
                stack.append(
                    jnp.concatenate(
                        [
                            done[(2 * p + t) * x_local : (2 * p + t + 1) * x_local, s : s + SEG]
                            for t in range(2)
                        ],
                        axis=1,
                    )
                )
            stack = jnp.concatenate(stack, axis=0)
            found = jnp.dot(
                hot_v[:, first_cell : first_cell + stack.shape[0]],
                stack,
                preferred_element_type=jnp.float32,
            )
            if k == 0:
                picked[p] = found
            else:
                picked[p] += found

    inputs[2].wait()
    for p in range(pairs):
        rows = picked[p].astype(jnp.bfloat16)
        both = jnp.dot(
            weights_v[p],
            jnp.concatenate([rows[:, :SEG], rows[:, SEG:]], axis=0),
            preferred_element_type=jnp.float32,
        )
        half = both.shape[0] // 2
        partial[:, place + p * group : place + (p + 1) * group] = (
            (both[:half] + both[half:])
            .reshape(partial.shape[0], group, SEG)
            .astype(jnp.bfloat16)
        )
    for copy in sent:
        copy.wait()


def y_sweep(swept, inverse, hot, weights, adjoint, befores, first, tests_total):
    sources, x_local, lanes = swept.shape
    pairs = lanes // SEG
    tests = 2 * pairs
    cells = inverse.shape[1]
    rows = hot.shape[0]
    group = weights.shape[1] // 2 // sources
    height = pairs * group + sum(before.shape[1] for before in befores)
    operands = [swept, inverse, hot, weights, *befores]
    in_specs = [ANY] * 4 + [VMEM] * len(befores)
    aliases = {}
    if adjoint is not None:
        aliases = {len(operands): 0}
        operands.append(adjoint)
        in_specs.append(ANY)
    return pl.pallas_call(
        functools.partial(y_kernel, first, len(befores)),
        in_specs=in_specs,
        out_specs=[ANY, VMEM],
        out_shape=[
            jax.ShapeDtypeStruct((tests_total, 1, x_local, cells), jnp.bfloat16),
            jax.ShapeDtypeStruct((sources, height, SEG), jnp.bfloat16),
        ],
        scratch_shapes=[
            pltpu.VMEM(swept.shape, swept.dtype),
            pltpu.VMEM(inverse.shape, inverse.dtype),
            pltpu.VMEM(hot.shape, hot.dtype),
            pltpu.VMEM(weights.shape, weights.dtype),
            pltpu.VMEM((tests * x_local, cells), jnp.bfloat16),
            pltpu.VMEM((tests, 1, x_local, cells), jnp.bfloat16),
            pltpu.VMEM((pairs, rows, 2 * SEG), jnp.float32),
            pltpu.SemaphoreType.DMA((3,)),
            pltpu.SemaphoreType.DMA((cells // BLOCK,)),
            pltpu.SemaphoreType.DMA((cells // BLOCK,)),
        ],
        input_output_aliases=aliases,
        compiler_params=params(LIMIT),
        cost_estimate=cost(2 * cells * tests * x_local * cells, 20 * MIB),
        name="y_sweep",
    )(*operands)


def body(heads, leak, x_inverse, y_inverse, misfit, row_owner, row_count, row_x, row_seg):
    tests, _, y_local, nx = heads.shape
    gx_count = lax.axis_size("gx")
    gz_count = lax.axis_size("gz")
    x_local = nx // gx_count
    ny = y_inverse.shape[1]
    ends = gz_count - 1
    up = [(i, i + 1) for i in range(ends)]
    down = [(i + 1, i) for i in range(ends)]

    spans = [(2 * sum(CHUNKS[:c]), 2 * size) for c, size in enumerate(CHUNKS)]
    arrived = []
    for first, size in spans:
        part = split(heads, first, size)
        arrived.append((lax.ppermute(part, "gz", down), lax.ppermute(part, "gz", up)))

    hot, *weights = prepare(
        misfit, row_owner, row_count, row_x, row_seg, x_local, ny // SEG, gx_count, gz_count
    )

    adjoint = None
    order = [hot, hot]
    partials = []
    for c, (first, size) in enumerate(spans):
        swept = x_sweep(heads, first, *arrived[c], leak, x_inverse, order[c])
        swept = swept.reshape(gx_count, x_local, size * y_local)
        swept = lax.all_to_all(swept, "gx", split_axis=0, concat_axis=0, tiled=True)
        befores = partials if c == len(spans) - 1 else []
        adjoint, partial = y_sweep(
            swept, y_inverse, hot, weights[c], adjoint, befores, first, tests
        )
        partials.append(partial)
        order.append(partial)

    sent = partials[-1].reshape(gx_count, tests, gz_count, SEG)
    sent = jnp.transpose(sent, (0, 2, 1, 3)).reshape(gx_count * gz_count, tests, SEG)
    got = lax.all_to_all(sent, ("gx", "gz"), split_axis=0, concat_axis=0, tiled=True)
    return (adjoint, jnp.sum(got.astype(jnp.float32), axis=0)[None])


def solution(mesh):
    placed = (
        P(None, "gz", "gx", None),
        P("gz", "gx", None),
        P("gz", None, None),
        P("gz", None, None),
        P(("gx", "gz"), None),
        P(("gx", "gz"), None),
        P(("gx", "gz")),
        P(("gx", "gz")),
        P(("gx", "gz")),
    )
    return jax.shard_map(
        body,
        mesh=mesh,
        in_specs=placed,
        out_specs=(P(None, "gz", "gx", None), P(("gx", "gz"), None, None)),
        check_vma=False,
    )
```

```python
import functools

import jax
import jax.numpy as jnp
from jax import lax
from jax.experimental import pallas as pl
from jax.experimental.pallas import tpu as pltpu
from jax.sharding import PartitionSpec as P

SEG = 128
CHUNKS = (2, 2, 2, 2)
BLOCK = 512
BLOCKS = 4
X_LIMIT = 52
Y_LIMIT = 52
LOAD_LIMIT = 50
RESIDENT_LIMIT = 44
NT = (((1,), (1,)), ((), ()))
MIB = 1 << 20
ANY = pl.BlockSpec(memory_space=pl.ANY)
VMEM = pl.BlockSpec(memory_space=pltpu.VMEM)
SMEM = pl.BlockSpec(memory_space=pltpu.SMEM)


def params(mib):
    return pltpu.CompilerParams(vmem_limit_bytes=mib * MIB)


def cost(flops, nbytes):
    return pl.CostEstimate(flops=flops, bytes_accessed=nbytes, transcendentals=0)


def fetch(source, buffer, sem):
    copy = pltpu.make_async_copy(source, buffer, sem)
    copy.start()
    return copy


def split_kernel(first, heads, *rest):
    out, buffer, sems = rest[-3:]
    fetch(heads.at[pl.ds(first, out.shape[0])], buffer, sems.at[0]).wait()
    fetch(buffer, out, sems.at[1]).wait()


def split(heads, first, size, after=()):
    return pl.pallas_call(
        functools.partial(split_kernel, first),
        in_specs=[ANY] * (1 + len(after)),
        out_specs=ANY,
        out_shape=jax.ShapeDtypeStruct((size,) + heads.shape[1:], heads.dtype),
        scratch_shapes=[
            pltpu.VMEM((size,) + heads.shape[1:], heads.dtype),
            pltpu.SemaphoreType.DMA((2,)),
        ],
        compiler_params=params(X_LIMIT),
        cost_estimate=cost(0, 2 * MIB),
        name="split",
    )(heads, *after)


def load_kernel(source, after, out, sem):
    fetch(source, out, sem).wait()


def load(inverse, after):
    return pl.pallas_call(
        load_kernel,
        in_specs=[ANY, ANY],
        out_specs=VMEM,
        out_shape=pltpu.VMEM(inverse.shape, inverse.dtype),
        scratch_shapes=[pltpu.SemaphoreType.DMA],
        compiler_params=params(LOAD_LIMIT),
        cost_estimate=cost(0, 16 * MIB),
        name="load",
    )(inverse, after)


def prepare_kernel(gz_count, count, misfit, owner, cells, after, hot, *weights):
    rows = owner.shape[1]
    lanes = lax.broadcasted_iota(jnp.int32, hot.shape, 1)
    hot[...] = (cells[...] == lanes).astype(jnp.float32).astype(jnp.bfloat16)

    m = weights[0].shape[1] // 2
    line = lax.broadcasted_iota(jnp.int32, (m, 2 * rows), 0)
    lane = lax.broadcasted_iota(jnp.int32, (m, 2 * rows), 1)
    test = (line // gz_count) % 2
    device = (line // (2 * gz_count)) * gz_count + line % gz_count
    owners = jnp.concatenate([owner[...], owner[...]], axis=1)
    keep = (owners == device) & (lane // rows == test) & (lane % rows < count[0])
    pair = 0
    for out in weights:
        for p in range(out.shape[0]):
            full = jnp.where(keep, misfit[pair : pair + 1], 0.0)
            high = full.astype(jnp.bfloat16)
            out[p, :m] = high
            out[p, m:] = (full - high.astype(jnp.float32)).astype(jnp.bfloat16)
            pair += 1


def prepare(
    misfit, row_owner, row_count, row_x, row_seg, x_local, segments, gx_count, gz_count, after
):
    rows, tests = misfit.shape
    m = 2 * gx_count * gz_count
    cell = (row_seg * x_local + row_x).reshape(rows, 1)
    return pl.pallas_call(
        functools.partial(prepare_kernel, gz_count),
        in_specs=[SMEM, VMEM, VMEM, VMEM, ANY],
        out_specs=[VMEM] * (1 + len(CHUNKS)),
        out_shape=[jax.ShapeDtypeStruct((rows, x_local * segments), jnp.bfloat16)]
        + [jax.ShapeDtypeStruct((size, 2 * m, 2 * rows), jnp.bfloat16) for size in CHUNKS],
        compiler_params=params(24),
        cost_estimate=cost(0, 6 * MIB),
        name="prepare",
    )(row_count, misfit.T.reshape(tests // 2, 2 * rows), row_owner.T, cell, after)


def x_kernel(first, waits, resident, ends, own, above, below, leak, inverse, *rest):
    out, own_v, above_v, below_v, leak_v, inverse_v, vertical, staged, sems, block_sems, out_sems = rest[
        waits:
    ]
    tests, _, lines, _ = own_v.shape
    cells = staged.shape[0]
    size = cells // BLOCKS
    leak_copy = fetch(leak, leak_v, sems.at[3 * tests])
    parts = [
        [
            fetch(own.at[pl.ds(first + t, 1)], own_v.at[pl.ds(t, 1)], sems.at[3 * t]),
            fetch(above.at[pl.ds(t, 1)], above_v.at[pl.ds(t, 1)], sems.at[3 * t + 1]),
            fetch(below.at[pl.ds(t, 1)], below_v.at[pl.ds(t, 1)], sems.at[3 * t + 2]),
        ]
        for t in range(tests)
    ]
    blocks = []

    def fetch_blocks(upto):
        for k in range(len(blocks), 0 if resident else min(upto, BLOCKS)):
            part = pl.ds(k * size, size)
            blocks.append(fetch(inverse.at[:, part], inverse_v.at[:, part], block_sems.at[k]))

    leak_copy.wait()
    for t in range(tests):
        for copy in parts[t]:
            copy.wait()
        fetch_blocks((t + 1) * BLOCKS // tests)
        centre = own_v[t, 0].astype(jnp.float32)
        near = above_v[t, 0].astype(jnp.float32) * ends[0] + below_v[t, 0].astype(jnp.float32) * ends[1]
        vertical[t * lines : (t + 1) * lines] = (
            centre + leak_v[0] * (near - 2.0 * centre)
        ).astype(jnp.bfloat16)
    fetch_blocks(BLOCKS)
    sent = []
    matrix = inverse if resident else inverse_v
    for k in range(BLOCKS):
        if not resident:
            blocks[k].wait()
        swept = lax.dot_general(
            vertical[...],
            matrix[0, k * size : (k + 1) * size],
            NT,
            preferred_element_type=jnp.float32,
        ).astype(jnp.bfloat16)
        staged[k * size : (k + 1) * size] = swept.T
        sent.append(
            fetch(staged.at[pl.ds(k * size, size)], out.at[pl.ds(k * size, size)], out_sems.at[k])
        )
    for copy in sent:
        copy.wait()


def x_sweep(own, first, above, below, leak, inverse, ends, after, resident):
    tests, _, lines, width = above.shape
    cells = inverse.shape[1]
    part = pltpu.VMEM(above.shape, above.dtype)
    return pl.pallas_call(
        functools.partial(x_kernel, first, len(after), resident),
        in_specs=[SMEM] + [ANY] * 4 + [VMEM if resident else ANY] + [ANY] * len(after),
        out_specs=ANY,
        out_shape=jax.ShapeDtypeStruct((cells, tests * lines), jnp.bfloat16),
        scratch_shapes=[
            part,
            part,
            part,
            pltpu.VMEM(leak.shape, leak.dtype),
            pltpu.VMEM((1, 8, 128) if resident else inverse.shape, inverse.dtype),
            pltpu.VMEM((tests * lines, width), jnp.bfloat16),
            pltpu.VMEM((cells, tests * lines), jnp.bfloat16),
            pltpu.SemaphoreType.DMA((3 * tests + 1,)),
            pltpu.SemaphoreType.DMA((BLOCKS,)),
            pltpu.SemaphoreType.DMA((BLOCKS,)),
        ],
        compiler_params=params(RESIDENT_LIMIT if resident else X_LIMIT),
        cost_estimate=cost(2 * cells * tests * lines * width, 20 * MIB),
        name="x_sweep",
    )(ends, own, above, below, leak, inverse, *after)


def y_kernel(first, earlier, swept, inverse, hot, weights, *rest):
    befores = rest[:earlier]
    out, partial, swept_v, inverse_v, hot_v, weights_v, lines, staged, picked, sems, block_sems, out_sems = rest[-12:]
    inputs = [
        fetch(source, buffer, sems.at[i])
        for i, (source, buffer) in enumerate(
            [(swept, swept_v), (hot, hot_v), (weights, weights_v)]
        )
    ]
    sources, x_local, lanes = swept_v.shape
    pairs = lanes // SEG
    tests = 2 * pairs
    y_local = SEG // 2
    cells = inverse_v.shape[1]
    blocks = [
        fetch(
            inverse.at[:, pl.ds(k, BLOCK)], inverse_v.at[:, pl.ds(k, BLOCK)], block_sems.at[k // BLOCK]
        )
        for k in range(0, cells, BLOCK)
    ]

    group = weights_v.shape[1] // 2 // sources
    place = 0
    for i, before in enumerate(befores):
        inputs.append(
            fetch(before, partial.at[:, pl.ds(place, before.shape[1])], sems.at[3 + i])
        )
        place += before.shape[1]

    inputs[0].wait()
    for p in range(pairs):
        for s in range(sources // 2):
            a = swept_v[2 * s, :, p * SEG : (p + 1) * SEG]
            b = swept_v[2 * s + 1, :, p * SEG : (p + 1) * SEG]
            for t in range(2):
                cut = slice(t * y_local, (t + 1) * y_local)
                lines[
                    (2 * p + t) * x_local : (2 * p + t + 1) * x_local,
                    s * SEG : (s + 1) * SEG,
                ] = jnp.concatenate([a[:, cut], b[:, cut]], axis=1)

    sent = []
    for k in range(0, cells, BLOCK):
        blocks[k // BLOCK].wait()
        done = lax.dot_general(
            lines[...], inverse_v[0, k : k + BLOCK], NT, preferred_element_type=jnp.float32
        ).astype(jnp.bfloat16)
        for t in range(tests):
            staged[t, 0, :, k : k + BLOCK] = done[t * x_local : (t + 1) * x_local]
        sent.append(
            fetch(
                staged.at[:, :, :, pl.ds(k, BLOCK)],
                out.at[pl.ds(first, tests), :, :, pl.ds(k, BLOCK)],
                out_sems.at[k // BLOCK],
            )
        )
        if k == 0:
            inputs[1].wait()
        first_cell = k // SEG * x_local
        for p in range(pairs):
            stack = []
            for s in range(0, BLOCK, SEG):
                stack.append(
                    jnp.concatenate(
                        [
                            done[(2 * p + t) * x_local : (2 * p + t + 1) * x_local, s : s + SEG]
                            for t in range(2)
                        ],
                        axis=1,
                    )
                )
            stack = jnp.concatenate(stack, axis=0)
            found = jnp.dot(
                hot_v[:, first_cell : first_cell + stack.shape[0]],
                stack,
                preferred_element_type=jnp.float32,
            )
            if k == 0:
                picked[p] = found
            else:
                picked[p] += found

    inputs[2].wait()
    for p in range(pairs):
        rows = picked[p].astype(jnp.bfloat16)
        both = jnp.dot(
            weights_v[p],
            jnp.concatenate([rows[:, :SEG], rows[:, SEG:]], axis=0),
            preferred_element_type=jnp.float32,
        )
        half = both.shape[0] // 2
        partial[:, place + p * group : place + (p + 1) * group] = (
            (both[:half] + both[half:])
            .reshape(partial.shape[0], group, SEG)
            .astype(jnp.bfloat16)
        )
    for copy in inputs[3:] + sent:
        copy.wait()


def y_sweep(swept, inverse, hot, weights, adjoint, befores, first, tests_total):
    sources, x_local, lanes = swept.shape
    pairs = lanes // SEG
    tests = 2 * pairs
    cells = inverse.shape[1]
    rows = hot.shape[0]
    group = weights.shape[1] // 2 // sources
    height = pairs * group + sum(before.shape[1] for before in befores)
    operands = [swept, inverse, hot, weights, *befores]
    in_specs = [ANY] * len(operands)
    aliases = {}
    if adjoint is not None:
        aliases = {len(operands): 0}
        operands.append(adjoint)
        in_specs.append(ANY)
    return pl.pallas_call(
        functools.partial(y_kernel, first, len(befores)),
        in_specs=in_specs,
        out_specs=[ANY, VMEM],
        out_shape=[
            jax.ShapeDtypeStruct((tests_total, 1, x_local, cells), jnp.bfloat16),
            jax.ShapeDtypeStruct((sources, height, SEG), jnp.bfloat16),
        ],
        scratch_shapes=[
            pltpu.VMEM(swept.shape, swept.dtype),
            pltpu.VMEM(inverse.shape, inverse.dtype),
            pltpu.VMEM(hot.shape, hot.dtype),
            pltpu.VMEM(weights.shape, weights.dtype),
            pltpu.VMEM((tests * x_local, cells), jnp.bfloat16),
            pltpu.VMEM((tests, 1, x_local, cells), jnp.bfloat16),
            pltpu.VMEM((pairs, rows, 2 * SEG), jnp.float32),
            pltpu.SemaphoreType.DMA((3 + len(befores),)),
            pltpu.SemaphoreType.DMA((cells // BLOCK,)),
            pltpu.SemaphoreType.DMA((cells // BLOCK,)),
        ],
        input_output_aliases=aliases,
        compiler_params=params(Y_LIMIT),
        cost_estimate=cost(2 * cells * tests * x_local * cells, 20 * MIB),
        name="y_sweep",
    )(*operands)


def body(heads, leak, x_inverse, y_inverse, misfit, row_owner, row_count, row_x, row_seg):
    tests, _, y_local, nx = heads.shape
    gx_count = lax.axis_size("gx")
    gz_count = lax.axis_size("gz")
    x_local = nx // gx_count
    ny = y_inverse.shape[1]
    up = [(i, (i + 1) % gz_count) for i in range(gz_count)]
    down = [((i + 1) % gz_count, i) for i in range(gz_count)]
    layer = lax.axis_index("gz")
    ends = jnp.stack([layer < gz_count - 1, layer > 0]).astype(jnp.float32)

    spans = [(2 * sum(CHUNKS[:c]), 2 * size) for c, size in enumerate(CHUNKS)]
    parts = [split(heads, *spans[0])]
    hot, *weights = prepare(
        misfit,
        row_owner,
        row_count,
        row_x,
        row_seg,
        x_local,
        ny // SEG,
        gx_count,
        gz_count,
        parts[0],
    )
    later = [split(heads, *span, after=[hot]) for span in spans[2:]]
    parts += [split(heads, *spans[1], after=later), *later]
    arrived = [(lax.ppermute(p, "gz", down), lax.ppermute(p, "gz", up)) for p in parts]
    adjoint = None
    order = [[hot], [], []]
    partials = []
    for c, (first, size) in enumerate(spans):
        swept = x_sweep(
            heads, first, *arrived[c], leak, x_inverse, ends, order[c], False
        )
        swept = swept.reshape(gx_count, x_local, size * y_local)
        swept = lax.all_to_all(swept, "gx", split_axis=0, concat_axis=0, tiled=True)
        befores = partials if c == len(spans) - 1 else []
        adjoint, partial = y_sweep(
            swept, y_inverse, hot, weights[c], adjoint, befores, first, tests
        )
        partials.append(partial)
        order.append([partial])

    sent = partials[-1].reshape(gx_count, tests, gz_count, SEG)
    sent = jnp.transpose(sent, (0, 2, 1, 3)).reshape(gx_count * gz_count, tests, SEG)
    got = lax.all_to_all(sent, ("gx", "gz"), split_axis=0, concat_axis=0, tiled=True)
    return (adjoint, jnp.sum(got.astype(jnp.float32), axis=0)[None])


def solution(mesh):
    placed = (
        P(None, "gz", "gx", None),
        P("gz", "gx", None),
        P("gz", None, None),
        P("gz", None, None),
        P(("gx", "gz"), None),
        P(("gx", "gz"), None),
        P(("gx", "gz")),
        P(("gx", "gz")),
        P(("gx", "gz")),
    )
    return jax.shard_map(
        body,
        mesh=mesh,
        in_specs=placed,
        out_specs=(P(None, "gz", "gx", None), P(("gx", "gz"), None, None)),
        check_vma=False,
    )
```

```python
import functools

import jax
import jax.numpy as jnp
from jax import lax
from jax.experimental import pallas as pl
from jax.experimental.pallas import tpu as pltpu
from jax.sharding import PartitionSpec as P

SEG = 128
CHUNKS = (2, 2, 2, 2)
BLOCK = 512
BLOCKS = 4
X_LIMIT = 52
Y_LIMIT = 52
LOAD_LIMIT = 50
RESIDENT_LIMIT = 24
RESIDENT = 1
LAST_LIMIT = 51
NT = (((1,), (1,)), ((), ()))
MIB = 1 << 20
ANY = pl.BlockSpec(memory_space=pl.ANY)
HBM = pl.BlockSpec(memory_space=pltpu.HBM)
VMEM = pl.BlockSpec(memory_space=pltpu.VMEM)
SMEM = pl.BlockSpec(memory_space=pltpu.SMEM)


def params(mib):
    return pltpu.CompilerParams(vmem_limit_bytes=mib * MIB)


def cost(flops, nbytes):
    return pl.CostEstimate(flops=flops, bytes_accessed=nbytes, transcendentals=0)


def fetch(source, buffer, sem):
    copy = pltpu.make_async_copy(source, buffer, sem)
    copy.start()
    return copy


def split_kernel(first, heads, *rest):
    out, buffer, sems = rest[-3:]
    fetch(heads.at[pl.ds(first, out.shape[0])], buffer, sems.at[0]).wait()
    fetch(buffer, out, sems.at[1]).wait()


def split(heads, first, size, after=(), limit=X_LIMIT):
    return pl.pallas_call(
        functools.partial(split_kernel, first),
        in_specs=[HBM] + [ANY] * len(after),
        out_specs=ANY,
        out_shape=jax.ShapeDtypeStruct((size,) + heads.shape[1:], heads.dtype),
        scratch_shapes=[
            pltpu.VMEM((size,) + heads.shape[1:], heads.dtype),
            pltpu.SemaphoreType.DMA((2,)),
        ],
        compiler_params=params(limit),
        cost_estimate=cost(0, 2 * MIB),
        name="split",
    )(heads, *after)


def load_kernel(source, after, out, sem):
    fetch(source, out, sem).wait()


def load(inverse, after):
    return pl.pallas_call(
        load_kernel,
        in_specs=[HBM, ANY],
        out_specs=VMEM,
        out_shape=pltpu.VMEM(inverse.shape, inverse.dtype),
        scratch_shapes=[pltpu.SemaphoreType.DMA],
        compiler_params=params(LOAD_LIMIT),
        cost_estimate=cost(0, 16 * MIB),
        name="load",
    )(inverse, after)


def prepare_kernel(gz_count, count, misfit, owner, cells, after, hot, *weights):
    rows = owner.shape[1]
    lanes = lax.broadcasted_iota(jnp.int32, hot.shape, 1)
    hot[...] = (cells[...] == lanes).astype(jnp.float32).astype(jnp.bfloat16)

    m = weights[0].shape[1] // 2
    line = lax.broadcasted_iota(jnp.int32, (m, 2 * rows), 0)
    lane = lax.broadcasted_iota(jnp.int32, (m, 2 * rows), 1)
    test = (line // gz_count) % 2
    device = (line // (2 * gz_count)) * gz_count + line % gz_count
    owners = jnp.concatenate([owner[...], owner[...]], axis=1)
    keep = (owners == device) & (lane // rows == test) & (lane % rows < count[0])
    pair = 0
    for out in weights:
        for p in range(out.shape[0]):
            full = jnp.where(keep, misfit[pair : pair + 1], 0.0)
            high = full.astype(jnp.bfloat16)
            out[p, :m] = high
            out[p, m:] = (full - high.astype(jnp.float32)).astype(jnp.bfloat16)
            pair += 1


def prepare(
    misfit, row_owner, row_count, row_x, row_seg, x_local, segments, gx_count, gz_count, after
):
    rows, tests = misfit.shape
    m = 2 * gx_count * gz_count
    cell = (row_seg * x_local + row_x).reshape(rows, 1)
    return pl.pallas_call(
        functools.partial(prepare_kernel, gz_count),
        in_specs=[SMEM, VMEM, VMEM, VMEM, ANY],
        out_specs=[VMEM] * (1 + len(CHUNKS)),
        out_shape=[jax.ShapeDtypeStruct((rows, x_local * segments), jnp.bfloat16)]
        + [jax.ShapeDtypeStruct((size, 2 * m, 2 * rows), jnp.bfloat16) for size in CHUNKS],
        compiler_params=params(24),
        cost_estimate=cost(0, 6 * MIB),
        name="prepare",
    )(row_count, misfit.T.reshape(tests // 2, 2 * rows), row_owner.T, cell, after)


def x_kernel(first, waits, resident, ends, own, above, below, leak, inverse, *rest):
    out, own_v, above_v, below_v, leak_v, inverse_v, vertical, staged, sems, block_sems, out_sems = rest[
        waits:
    ]
    tests, _, lines, _ = own_v.shape
    cells = staged.shape[0]
    size = cells // BLOCKS
    leak_copy = fetch(leak, leak_v, sems.at[3 * tests])
    parts = [
        [
            fetch(own.at[pl.ds(first + t, 1)], own_v.at[pl.ds(t, 1)], sems.at[3 * t]),
            fetch(above.at[pl.ds(t, 1)], above_v.at[pl.ds(t, 1)], sems.at[3 * t + 1]),
            fetch(below.at[pl.ds(t, 1)], below_v.at[pl.ds(t, 1)], sems.at[3 * t + 2]),
        ]
        for t in range(tests)
    ]
    blocks = []

    def fetch_blocks(upto):
        for k in range(len(blocks), 0 if resident else min(upto, BLOCKS)):
            part = pl.ds(k * size, size)
            blocks.append(fetch(inverse.at[:, part], inverse_v.at[:, part], block_sems.at[k]))

    leak_copy.wait()
    for t in range(tests):
        for copy in parts[t]:
            copy.wait()
        fetch_blocks((t + 1) * BLOCKS // tests)
        centre = own_v[t, 0].astype(jnp.float32)
        near = above_v[t, 0].astype(jnp.float32) * ends[0] + below_v[t, 0].astype(jnp.float32) * ends[1]
        vertical[t * lines : (t + 1) * lines] = (
            centre + leak_v[0] * (near - 2.0 * centre)
        ).astype(jnp.bfloat16)
    fetch_blocks(BLOCKS)
    sent = []
    matrix = inverse if resident else inverse_v
    for k in range(BLOCKS):
        if not resident:
            blocks[k].wait()
        part = matrix[0, k * size : (k + 1) * size]
        if resident:
            staged[k * size : (k + 1) * size] = lax.dot_general(
                part, vertical[...], NT, preferred_element_type=jnp.float32
            ).astype(jnp.bfloat16)
        else:
            staged[k * size : (k + 1) * size] = (
                lax.dot_general(vertical[...], part, NT, preferred_element_type=jnp.float32)
                .astype(jnp.bfloat16)
                .T
            )
        sent.append(
            fetch(staged.at[pl.ds(k * size, size)], out.at[pl.ds(k * size, size)], out_sems.at[k])
        )
    for copy in sent:
        copy.wait()


def x_sweep(own, first, above, below, leak, inverse, ends, after, resident):
    tests, _, lines, width = above.shape
    cells = inverse.shape[1]
    part = pltpu.VMEM(above.shape, above.dtype)
    return pl.pallas_call(
        functools.partial(x_kernel, first, len(after), resident),
        in_specs=[SMEM, HBM, ANY, ANY, HBM, VMEM if resident else HBM] + [ANY] * len(after),
        out_specs=HBM,
        out_shape=pltpu.HBM((cells, tests * lines), jnp.bfloat16),
        scratch_shapes=[
            part,
            part,
            part,
            pltpu.VMEM(leak.shape, leak.dtype),
            pltpu.VMEM((1, 8, 128) if resident else inverse.shape, inverse.dtype),
            pltpu.VMEM((tests * lines, width), jnp.bfloat16),
            pltpu.VMEM((cells, tests * lines), jnp.bfloat16),
            pltpu.SemaphoreType.DMA((3 * tests + 1,)),
            pltpu.SemaphoreType.DMA((BLOCKS,)),
            pltpu.SemaphoreType.DMA((BLOCKS,)),
        ],
        compiler_params=params(RESIDENT_LIMIT if resident else X_LIMIT),
        cost_estimate=cost(2 * cells * tests * lines * width, 20 * MIB),
        name="x_sweep",
    )(ends, own, above, below, leak, inverse, *after)


def y_kernel(first, earlier, swept, inverse, hot, weights, *rest):
    befores = rest[:earlier]
    out, partial, swept_v, inverse_v, hot_v, weights_v, lines, staged, picked, sems, block_sems, out_sems = rest[-12:]
    inputs = [
        fetch(source, buffer, sems.at[i])
        for i, (source, buffer) in enumerate(
            [(swept, swept_v), (hot, hot_v), (weights, weights_v)]
        )
    ]
    sources, x_local, lanes = swept_v.shape
    pairs = lanes // SEG
    tests = 2 * pairs
    y_local = SEG // 2
    cells = inverse_v.shape[1]
    blocks = [
        fetch(
            inverse.at[:, pl.ds(k, BLOCK)], inverse_v.at[:, pl.ds(k, BLOCK)], block_sems.at[k // BLOCK]
        )
        for k in range(0, cells, BLOCK)
    ]

    group = weights_v.shape[1] // 2 // sources
    place = 0
    for i, before in enumerate(befores):
        inputs.append(
            fetch(before, partial.at[:, pl.ds(place, before.shape[1])], sems.at[3 + i])
        )
        place += before.shape[1]

    inputs[0].wait()
    for p in range(pairs):
        for s in range(sources // 2):
            a = swept_v[2 * s, :, p * SEG : (p + 1) * SEG]
            b = swept_v[2 * s + 1, :, p * SEG : (p + 1) * SEG]
            for t in range(2):
                cut = slice(t * y_local, (t + 1) * y_local)
                lines[
                    (2 * p + t) * x_local : (2 * p + t + 1) * x_local,
                    s * SEG : (s + 1) * SEG,
                ] = jnp.concatenate([a[:, cut], b[:, cut]], axis=1)

    sent = []
    for k in range(0, cells, BLOCK):
        blocks[k // BLOCK].wait()
        done = lax.dot_general(
            lines[...], inverse_v[0, k : k + BLOCK], NT, preferred_element_type=jnp.float32
        ).astype(jnp.bfloat16)
        for t in range(tests):
            staged[t, 0, :, k : k + BLOCK] = done[t * x_local : (t + 1) * x_local]
        sent.append(
            fetch(
                staged.at[:, :, :, pl.ds(k, BLOCK)],
                out.at[pl.ds(first, tests), :, :, pl.ds(k, BLOCK)],
                out_sems.at[k // BLOCK],
            )
        )
        if k == 0:
            inputs[1].wait()
        first_cell = k // SEG * x_local
        for p in range(pairs):
            stack = []
            for s in range(0, BLOCK, SEG):
                stack.append(
                    jnp.concatenate(
                        [
                            done[(2 * p + t) * x_local : (2 * p + t + 1) * x_local, s : s + SEG]
                            for t in range(2)
                        ],
                        axis=1,
                    )
                )
            stack = jnp.concatenate(stack, axis=0)
            found = jnp.dot(
                hot_v[:, first_cell : first_cell + stack.shape[0]],
                stack,
                preferred_element_type=jnp.float32,
            )
            if k == 0:
                picked[p] = found
            else:
                picked[p] += found

    inputs[2].wait()
    for p in range(pairs):
        rows = picked[p].astype(jnp.bfloat16)
        both = jnp.dot(
            weights_v[p],
            jnp.concatenate([rows[:, :SEG], rows[:, SEG:]], axis=0),
            preferred_element_type=jnp.float32,
        )
        half = both.shape[0] // 2
        partial[:, place + p * group : place + (p + 1) * group] = (
            (both[:half] + both[half:])
            .reshape(partial.shape[0], group, SEG)
            .astype(jnp.bfloat16)
        )
    for copy in inputs[3:] + sent:
        copy.wait()


def y_sweep(swept, inverse, hot, weights, adjoint, befores, first, tests_total, limit):
    sources, x_local, lanes = swept.shape
    pairs = lanes // SEG
    tests = 2 * pairs
    cells = inverse.shape[1]
    rows = hot.shape[0]
    group = weights.shape[1] // 2 // sources
    height = pairs * group + sum(before.shape[1] for before in befores)
    operands = [swept, inverse, hot, weights, *befores]
    in_specs = [ANY] + [HBM] * 3 + [ANY] * len(befores)
    aliases = {}
    if adjoint is not None:
        aliases = {len(operands): 0}
        operands.append(adjoint)
        in_specs.append(ANY)
    return pl.pallas_call(
        functools.partial(y_kernel, first, len(befores)),
        in_specs=in_specs,
        out_specs=[ANY, VMEM],
        out_shape=[
            jax.ShapeDtypeStruct((tests_total, 1, x_local, cells), jnp.bfloat16),
            jax.ShapeDtypeStruct((sources, height, SEG), jnp.bfloat16),
        ],
        scratch_shapes=[
            pltpu.VMEM(swept.shape, swept.dtype),
            pltpu.VMEM(inverse.shape, inverse.dtype),
            pltpu.VMEM(hot.shape, hot.dtype),
            pltpu.VMEM(weights.shape, weights.dtype),
            pltpu.VMEM((tests * x_local, cells), jnp.bfloat16),
            pltpu.VMEM((tests, 1, x_local, cells), jnp.bfloat16),
            pltpu.VMEM((pairs, rows, 2 * SEG), jnp.float32),
            pltpu.SemaphoreType.DMA((3 + len(befores),)),
            pltpu.SemaphoreType.DMA((cells // BLOCK,)),
            pltpu.SemaphoreType.DMA((cells // BLOCK,)),
        ],
        input_output_aliases=aliases,
        compiler_params=params(limit),
        cost_estimate=cost(2 * cells * tests * x_local * cells, 20 * MIB),
        name="y_sweep",
    )(*operands)


def body(heads, leak, x_inverse, y_inverse, misfit, row_owner, row_count, row_x, row_seg):
    tests, _, y_local, nx = heads.shape
    gx_count = lax.axis_size("gx")
    gz_count = lax.axis_size("gz")
    x_local = nx // gx_count
    ny = y_inverse.shape[1]
    up = [(i, (i + 1) % gz_count) for i in range(gz_count)]
    down = [((i + 1) % gz_count, i) for i in range(gz_count)]
    layer = lax.axis_index("gz")
    ends = jnp.stack([layer < gz_count - 1, layer > 0]).astype(jnp.float32)

    spans = [(2 * sum(CHUNKS[:c]), 2 * size) for c, size in enumerate(CHUNKS)]
    parts = [split(heads, *spans[0])]
    hot, *weights = prepare(
        misfit,
        row_owner,
        row_count,
        row_x,
        row_seg,
        x_local,
        ny // SEG,
        gx_count,
        gz_count,
        parts[0],
    )
    later = [split(heads, *span, after=[hot]) for span in spans[2:]]
    parts += [split(heads, *spans[1], after=later), *later]
    arrived = [(lax.ppermute(p, "gz", down), lax.ppermute(p, "gz", up)) for p in parts]
    adjoint = None
    order = [[hot], [], []]
    partials = []
    for c, (first, size) in enumerate(spans):
        resident = c < RESIDENT
        matrix = load(x_inverse, parts[1] if c == 0 else lines) if resident else x_inverse
        lines = x_sweep(heads, first, *arrived[c], leak, matrix, ends, order[c], resident)
        swept = lines.reshape(gx_count, x_local, size * y_local)
        swept = lax.all_to_all(swept, "gx", split_axis=0, concat_axis=0, tiled=True)
        befores = partials if c == len(spans) - 1 else []
        adjoint, partial = y_sweep(
            swept,
            y_inverse,
            hot,
            weights[c],
            adjoint,
            befores,
            first,
            tests,
            LAST_LIMIT if befores else Y_LIMIT,
        )
        partials.append(partial)
        order.append([partial])

    sent = partials[-1].reshape(gx_count, tests, gz_count, SEG)
    sent = jnp.transpose(sent, (0, 2, 1, 3)).reshape(gx_count * gz_count, tests, SEG)
    got = lax.all_to_all(sent, ("gx", "gz"), split_axis=0, concat_axis=0, tiled=True)
    return (adjoint, jnp.sum(got.astype(jnp.float32), axis=0)[None])


def solution(mesh):
    placed = (
        P(None, "gz", "gx", None),
        P("gz", "gx", None),
        P("gz", None, None),
        P("gz", None, None),
        P(("gx", "gz"), None),
        P(("gx", "gz"), None),
        P(("gx", "gz")),
        P(("gx", "gz")),
        P(("gx", "gz")),
    )
    return jax.shard_map(
        body,
        mesh=mesh,
        in_specs=placed,
        out_specs=(P(None, "gz", "gx", None), P(("gx", "gz"), None, None)),
        check_vma=False,
    )
```

```python
import functools

import jax
import jax.numpy as jnp
from jax import lax
from jax.experimental import pallas as pl
from jax.experimental.pallas import tpu as pltpu
from jax.sharding import PartitionSpec as P

SEG = 128
CHUNKS = (2, 2, 2, 2)
BLOCK = 512
BLOCKS = 4
X_LIMIT = 52
Y_LIMIT = 52
LOAD_LIMIT = 50
RESIDENT_LIMIT = 24
RESIDENT = 2
LAST_LIMIT = 51
NT = (((1,), (1,)), ((), ()))
MIB = 1 << 20
SCALE = 1
ANY = pl.BlockSpec(memory_space=pl.ANY)
HBM = pl.BlockSpec(memory_space=pltpu.HBM)
VMEM = pl.BlockSpec(memory_space=pltpu.VMEM)
SMEM = pl.BlockSpec(memory_space=pltpu.SMEM)


def params(mib):
    return pltpu.CompilerParams(vmem_limit_bytes=mib * MIB)


def cost(flops, nbytes):
    return pl.CostEstimate(flops=flops // SCALE, bytes_accessed=nbytes // SCALE, transcendentals=0)


def fetch(source, buffer, sem):
    copy = pltpu.make_async_copy(source, buffer, sem)
    copy.start()
    return copy


def split_kernel(first, heads, *rest):
    out, buffer, sems = rest[-3:]
    fetch(heads.at[pl.ds(first, out.shape[0])], buffer, sems.at[0]).wait()
    fetch(buffer, out, sems.at[1]).wait()


def split(heads, first, size, after=(), limit=X_LIMIT, space=jax.ShapeDtypeStruct):
    return pl.pallas_call(
        functools.partial(split_kernel, first),
        in_specs=[HBM] + [ANY] * len(after),
        out_specs=ANY,
        out_shape=space((size,) + heads.shape[1:], heads.dtype),
        scratch_shapes=[
            pltpu.VMEM((size,) + heads.shape[1:], heads.dtype),
            pltpu.SemaphoreType.DMA((2,)),
        ],
        compiler_params=params(limit),
        cost_estimate=cost(0, 2 * MIB),
        name="split",
    )(heads, *after)


def load_kernel(source, after, out, sem):
    fetch(source, out, sem).wait()


def load(inverse, after):
    return pl.pallas_call(
        load_kernel,
        in_specs=[HBM, ANY],
        out_specs=VMEM,
        out_shape=pltpu.VMEM(inverse.shape, inverse.dtype),
        scratch_shapes=[pltpu.SemaphoreType.DMA],
        compiler_params=params(LOAD_LIMIT),
        cost_estimate=cost(0, 16 * MIB),
        name="load",
    )(inverse, after)


def prepare_kernel(gz_count, count, misfit, owner, cells, after, hot, *weights):
    rows = owner.shape[1]
    lanes = lax.broadcasted_iota(jnp.int32, hot.shape, 1)
    hot[...] = (cells[...] == lanes).astype(jnp.float32).astype(jnp.bfloat16)

    m = weights[0].shape[1] // 2
    line = lax.broadcasted_iota(jnp.int32, (m, 2 * rows), 0)
    lane = lax.broadcasted_iota(jnp.int32, (m, 2 * rows), 1)
    test = (line // gz_count) % 2
    device = (line // (2 * gz_count)) * gz_count + line % gz_count
    owners = jnp.concatenate([owner[...], owner[...]], axis=1)
    keep = (owners == device) & (lane // rows == test) & (lane % rows < count[0])
    pair = 0
    for out in weights:
        for p in range(out.shape[0]):
            full = jnp.where(keep, misfit[pair : pair + 1], 0.0)
            high = full.astype(jnp.bfloat16)
            out[p, :m] = high
            out[p, m:] = (full - high.astype(jnp.float32)).astype(jnp.bfloat16)
            pair += 1


def prepare(
    misfit, row_owner, row_count, row_x, row_seg, x_local, segments, gx_count, gz_count, after
):
    rows, tests = misfit.shape
    m = 2 * gx_count * gz_count
    cell = (row_seg * x_local + row_x).reshape(rows, 1)
    return pl.pallas_call(
        functools.partial(prepare_kernel, gz_count),
        in_specs=[SMEM, VMEM, VMEM, VMEM, ANY],
        out_specs=[VMEM] * (1 + len(CHUNKS)),
        out_shape=[jax.ShapeDtypeStruct((rows, x_local * segments), jnp.bfloat16)]
        + [jax.ShapeDtypeStruct((size, 2 * m, 2 * rows), jnp.bfloat16) for size in CHUNKS],
        compiler_params=params(24),
        cost_estimate=cost(0, 6 * MIB),
        name="prepare",
    )(row_count, misfit.T.reshape(tests // 2, 2 * rows), row_owner.T, cell, after)


def x_kernel(first, waits, resident, ends, own, above, below, leak, inverse, *rest):
    out, own_v, above_v, below_v, leak_v, inverse_v, vertical, staged, sems, block_sems, out_sems = rest[
        waits:
    ]
    tests, _, lines, _ = own_v.shape
    cells = staged.shape[0]
    size = cells // BLOCKS
    leak_copy = fetch(leak, leak_v, sems.at[3 * tests])
    parts = [
        [
            fetch(own.at[pl.ds(first + t, 1)], own_v.at[pl.ds(t, 1)], sems.at[3 * t]),
            fetch(above.at[pl.ds(t, 1)], above_v.at[pl.ds(t, 1)], sems.at[3 * t + 1]),
            fetch(below.at[pl.ds(t, 1)], below_v.at[pl.ds(t, 1)], sems.at[3 * t + 2]),
        ]
        for t in range(tests)
    ]
    blocks = []

    def fetch_blocks(upto):
        for k in range(len(blocks), 0 if resident else min(upto, BLOCKS)):
            part = pl.ds(k * size, size)
            blocks.append(fetch(inverse.at[:, part], inverse_v.at[:, part], block_sems.at[k]))

    leak_copy.wait()
    for t in range(tests):
        for copy in parts[t]:
            copy.wait()
        fetch_blocks((t + 1) * BLOCKS // tests)
        centre = own_v[t, 0].astype(jnp.float32)
        near = above_v[t, 0].astype(jnp.float32) * ends[0] + below_v[t, 0].astype(jnp.float32) * ends[1]
        vertical[t * lines : (t + 1) * lines] = (
            centre + leak_v[0] * (near - 2.0 * centre)
        ).astype(jnp.bfloat16)
    fetch_blocks(BLOCKS)
    sent = []
    matrix = inverse if resident else inverse_v
    for k in range(BLOCKS):
        if not resident:
            blocks[k].wait()
        part = matrix[0, k * size : (k + 1) * size]
        if resident:
            staged[k * size : (k + 1) * size] = lax.dot_general(
                part, vertical[...], NT, preferred_element_type=jnp.float32
            ).astype(jnp.bfloat16)
        else:
            staged[k * size : (k + 1) * size] = (
                lax.dot_general(vertical[...], part, NT, preferred_element_type=jnp.float32)
                .astype(jnp.bfloat16)
                .T
            )
        sent.append(
            fetch(staged.at[pl.ds(k * size, size)], out.at[pl.ds(k * size, size)], out_sems.at[k])
        )
    for copy in sent:
        copy.wait()


def x_sweep(own, first, above, below, leak, inverse, ends, after, resident):
    tests, _, lines, width = above.shape
    cells = inverse.shape[1]
    part = pltpu.VMEM(above.shape, above.dtype)
    return pl.pallas_call(
        functools.partial(x_kernel, first, len(after), resident),
        in_specs=[SMEM, HBM, ANY, ANY, HBM, VMEM if resident else HBM] + [ANY] * len(after),
        out_specs=HBM,
        out_shape=pltpu.HBM((cells, tests * lines), jnp.bfloat16),
        scratch_shapes=[
            part,
            part,
            part,
            pltpu.VMEM(leak.shape, leak.dtype),
            pltpu.VMEM((1, 8, 128) if resident else inverse.shape, inverse.dtype),
            pltpu.VMEM((tests * lines, width), jnp.bfloat16),
            pltpu.VMEM((cells, tests * lines), jnp.bfloat16),
            pltpu.SemaphoreType.DMA((3 * tests + 1,)),
            pltpu.SemaphoreType.DMA((BLOCKS,)),
            pltpu.SemaphoreType.DMA((BLOCKS,)),
        ],
        compiler_params=params(RESIDENT_LIMIT if resident else X_LIMIT),
        cost_estimate=cost(2 * cells * tests * lines * width, 20 * MIB),
        name="x_sweep",
    )(ends, own, above, below, leak, inverse, *after)


def y_kernel(first, earlier, swept, inverse, hot, weights, *rest):
    befores = rest[:earlier]
    out, partial, swept_v, inverse_v, hot_v, weights_v, lines, staged, picked, sems, block_sems, out_sems = rest[-12:]
    inputs = [
        fetch(source, buffer, sems.at[i])
        for i, (source, buffer) in enumerate(
            [(swept, swept_v), (hot, hot_v), (weights, weights_v)]
        )
    ]
    sources, x_local, lanes = swept_v.shape
    pairs = lanes // SEG
    tests = 2 * pairs
    y_local = SEG // 2
    cells = inverse_v.shape[1]
    blocks = [
        fetch(
            inverse.at[:, pl.ds(k, BLOCK)], inverse_v.at[:, pl.ds(k, BLOCK)], block_sems.at[k // BLOCK]
        )
        for k in range(0, cells, BLOCK)
    ]

    group = weights_v.shape[1] // 2 // sources
    place = 0
    for i, before in enumerate(befores):
        inputs.append(
            fetch(before, partial.at[:, pl.ds(place, before.shape[1])], sems.at[3 + i])
        )
        place += before.shape[1]

    inputs[0].wait()
    for p in range(pairs):
        for s in range(sources // 2):
            a = swept_v[2 * s, :, p * SEG : (p + 1) * SEG]
            b = swept_v[2 * s + 1, :, p * SEG : (p + 1) * SEG]
            for t in range(2):
                cut = slice(t * y_local, (t + 1) * y_local)
                lines[
                    (2 * p + t) * x_local : (2 * p + t + 1) * x_local,
                    s * SEG : (s + 1) * SEG,
                ] = jnp.concatenate([a[:, cut], b[:, cut]], axis=1)

    sent = []
    for k in range(0, cells, BLOCK):
        blocks[k // BLOCK].wait()
        done = lax.dot_general(
            lines[...], inverse_v[0, k : k + BLOCK], NT, preferred_element_type=jnp.float32
        ).astype(jnp.bfloat16)
        for t in range(tests):
            staged[t, 0, :, k : k + BLOCK] = done[t * x_local : (t + 1) * x_local]
        sent.append(
            fetch(
                staged.at[:, :, :, pl.ds(k, BLOCK)],
                out.at[pl.ds(first, tests), :, :, pl.ds(k, BLOCK)],
                out_sems.at[k // BLOCK],
            )
        )
        if k == 0:
            inputs[1].wait()
        first_cell = k // SEG * x_local
        for p in range(pairs):
            stack = []
            for s in range(0, BLOCK, SEG):
                stack.append(
                    jnp.concatenate(
                        [
                            done[(2 * p + t) * x_local : (2 * p + t + 1) * x_local, s : s + SEG]
                            for t in range(2)
                        ],
                        axis=1,
                    )
                )
            stack = jnp.concatenate(stack, axis=0)
            found = jnp.dot(
                hot_v[:, first_cell : first_cell + stack.shape[0]],
                stack,
                preferred_element_type=jnp.float32,
            )
            if k == 0:
                picked[p] = found
            else:
                picked[p] += found

    inputs[2].wait()
    for p in range(pairs):
        rows = picked[p].astype(jnp.bfloat16)
        both = jnp.dot(
            weights_v[p],
            jnp.concatenate([rows[:, :SEG], rows[:, SEG:]], axis=0),
            preferred_element_type=jnp.float32,
        )
        half = both.shape[0] // 2
        partial[:, place + p * group : place + (p + 1) * group] = (
            (both[:half] + both[half:])
            .reshape(partial.shape[0], group, SEG)
            .astype(jnp.bfloat16)
        )
    for copy in inputs[3:] + sent:
        copy.wait()


def y_sweep(swept, inverse, hot, weights, adjoint, befores, first, tests_total, limit):
    sources, x_local, lanes = swept.shape
    pairs = lanes // SEG
    tests = 2 * pairs
    cells = inverse.shape[1]
    rows = hot.shape[0]
    group = weights.shape[1] // 2 // sources
    height = pairs * group + sum(before.shape[1] for before in befores)
    operands = [swept, inverse, hot, weights, *befores]
    in_specs = [ANY] + [HBM] * 3 + [ANY] * len(befores)
    aliases = {}
    if adjoint is not None:
        aliases = {len(operands): 0}
        operands.append(adjoint)
        in_specs.append(ANY)
    return pl.pallas_call(
        functools.partial(y_kernel, first, len(befores)),
        in_specs=in_specs,
        out_specs=[ANY, VMEM],
        out_shape=[
            jax.ShapeDtypeStruct((tests_total, 1, x_local, cells), jnp.bfloat16),
            jax.ShapeDtypeStruct((sources, height, SEG), jnp.bfloat16),
        ],
        scratch_shapes=[
            pltpu.VMEM(swept.shape, swept.dtype),
            pltpu.VMEM(inverse.shape, inverse.dtype),
            pltpu.VMEM(hot.shape, hot.dtype),
            pltpu.VMEM(weights.shape, weights.dtype),
            pltpu.VMEM((tests * x_local, cells), jnp.bfloat16),
            pltpu.VMEM((tests, 1, x_local, cells), jnp.bfloat16),
            pltpu.VMEM((pairs, rows, 2 * SEG), jnp.float32),
            pltpu.SemaphoreType.DMA((3 + len(befores),)),
            pltpu.SemaphoreType.DMA((cells // BLOCK,)),
            pltpu.SemaphoreType.DMA((cells // BLOCK,)),
        ],
        input_output_aliases=aliases,
        compiler_params=params(limit),
        cost_estimate=cost(2 * cells * tests * x_local * cells, 20 * MIB),
        name="y_sweep",
    )(*operands)


def body(heads, leak, x_inverse, y_inverse, misfit, row_owner, row_count, row_x, row_seg):
    tests, _, y_local, nx = heads.shape
    gx_count = lax.axis_size("gx")
    gz_count = lax.axis_size("gz")
    x_local = nx // gx_count
    ny = y_inverse.shape[1]
    up = [(i, (i + 1) % gz_count) for i in range(gz_count)]
    down = [((i + 1) % gz_count, i) for i in range(gz_count)]
    layer = lax.axis_index("gz")
    ends = jnp.stack([layer < gz_count - 1, layer > 0]).astype(jnp.float32)

    spans = [(2 * sum(CHUNKS[:c]), 2 * size) for c, size in enumerate(CHUNKS)]
    parts = [split(heads, *spans[0], space=pltpu.VMEM)]
    hot, *weights = prepare(
        misfit,
        row_owner,
        row_count,
        row_x,
        row_seg,
        x_local,
        ny // SEG,
        gx_count,
        gz_count,
        parts[0],
    )
    later = [split(heads, *span, after=[hot]) for span in spans[2:]]
    parts += [split(heads, *spans[1], after=[hot]), *later]
    below = [lax.ppermute(p, "gz", up) for p in parts]
    arrived = [(lax.ppermute(p, "gz", down), b) for p, b in zip(parts, below)]
    adjoint = None
    order = [[hot, *parts[2:]], [], []]
    partials = []
    for c, (first, size) in enumerate(spans):
        resident = c < RESIDENT
        matrix = load(x_inverse, parts[c + 1]) if resident else x_inverse
        own, place = (parts[c], 0) if resident else (heads, first)
        lines = x_sweep(own, place, *arrived[c], leak, matrix, ends, order[c], resident)
        swept = lines.reshape(gx_count, x_local, size * y_local)
        swept = lax.all_to_all(swept, "gx", split_axis=0, concat_axis=0, tiled=True)
        befores = partials if c == len(spans) - 1 else []
        adjoint, partial = y_sweep(
            swept,
            y_inverse,
            hot,
            weights[c],
            adjoint,
            befores,
            first,
            tests,
            LAST_LIMIT if befores else Y_LIMIT,
        )
        partials.append(partial)
        order.append([partial])

    sent = partials[-1].reshape(gx_count, tests, gz_count, SEG)
    sent = jnp.transpose(sent, (0, 2, 1, 3)).reshape(gx_count * gz_count, tests, SEG)
    got = lax.all_to_all(sent, ("gx", "gz"), split_axis=0, concat_axis=0, tiled=True)
    return (adjoint, jnp.sum(got.astype(jnp.float32), axis=0)[None])


def solution(mesh):
    placed = (
        P(None, "gz", "gx", None),
        P("gz", "gx", None),
        P("gz", None, None),
        P("gz", None, None),
        P(("gx", "gz"), None),
        P(("gx", "gz"), None),
        P(("gx", "gz")),
        P(("gx", "gz")),
        P(("gx", "gz")),
    )
    return jax.shard_map(
        body,
        mesh=mesh,
        in_specs=placed,
        out_specs=(P(None, "gz", "gx", None), P(("gx", "gz"), None, None)),
        check_vma=False,
    )
```

```python
import functools

import jax
import jax.numpy as jnp
from jax import lax
from jax.experimental import pallas as pl
from jax.experimental.pallas import tpu as pltpu
from jax.sharding import PartitionSpec as P

SEG = 128
CHUNKS = (2, 2, 2, 2)
BLOCK = 512
BLOCKS = 4
X_LIMIT = 52
Y_LIMIT = 52
LOAD_LIMIT = 50
RESIDENT_LIMIT = 24
RESIDENT = 3
LAST_LIMIT = 51
NT = (((1,), (1,)), ((), ()))
MIB = 1 << 20
SCALE = 1
ANY = pl.BlockSpec(memory_space=pl.ANY)
HBM = pl.BlockSpec(memory_space=pltpu.HBM)
VMEM = pl.BlockSpec(memory_space=pltpu.VMEM)
SMEM = pl.BlockSpec(memory_space=pltpu.SMEM)


def params(mib):
    return pltpu.CompilerParams(vmem_limit_bytes=mib * MIB)


def cost(flops, nbytes):
    return pl.CostEstimate(flops=flops // SCALE, bytes_accessed=nbytes // SCALE, transcendentals=0)


def fetch(source, buffer, sem):
    copy = pltpu.make_async_copy(source, buffer, sem)
    copy.start()
    return copy


def split_kernel(first, heads, *rest):
    out, buffer, sems = rest[-3:]
    fetch(heads.at[pl.ds(first, out.shape[0])], buffer, sems.at[0]).wait()
    fetch(buffer, out, sems.at[1]).wait()


def split(heads, first, size, after=(), limit=X_LIMIT, space=jax.ShapeDtypeStruct):
    return pl.pallas_call(
        functools.partial(split_kernel, first),
        in_specs=[HBM] + [ANY] * len(after),
        out_specs=ANY,
        out_shape=space((size,) + heads.shape[1:], heads.dtype),
        scratch_shapes=[
            pltpu.VMEM((size,) + heads.shape[1:], heads.dtype),
            pltpu.SemaphoreType.DMA((2,)),
        ],
        compiler_params=params(limit),
        cost_estimate=cost(0, 2 * MIB),
        name="split",
    )(heads, *after)


def load_kernel(source, after, out, sem):
    fetch(source, out, sem).wait()


def load(inverse, after):
    return pl.pallas_call(
        load_kernel,
        in_specs=[HBM, ANY],
        out_specs=VMEM,
        out_shape=pltpu.VMEM(inverse.shape, inverse.dtype),
        scratch_shapes=[pltpu.SemaphoreType.DMA],
        compiler_params=params(LOAD_LIMIT),
        cost_estimate=cost(0, 16 * MIB),
        name="load",
    )(inverse, after)


def prepare_kernel(gz_count, count, misfit, owner, cells, after, hot, *weights):
    rows = owner.shape[1]
    lanes = lax.broadcasted_iota(jnp.int32, hot.shape, 1)
    hot[...] = (cells[...] == lanes).astype(jnp.float32).astype(jnp.bfloat16)

    m = weights[0].shape[1] // 2
    line = lax.broadcasted_iota(jnp.int32, (m, 2 * rows), 0)
    lane = lax.broadcasted_iota(jnp.int32, (m, 2 * rows), 1)
    test = (line // gz_count) % 2
    device = (line // (2 * gz_count)) * gz_count + line % gz_count
    owners = jnp.concatenate([owner[...], owner[...]], axis=1)
    keep = (owners == device) & (lane // rows == test) & (lane % rows < count[0])
    pair = 0
    for out in weights:
        for p in range(out.shape[0]):
            full = jnp.where(keep, misfit[pair : pair + 1], 0.0)
            high = full.astype(jnp.bfloat16)
            out[p, :m] = high
            out[p, m:] = (full - high.astype(jnp.float32)).astype(jnp.bfloat16)
            pair += 1


def prepare(
    misfit, row_owner, row_count, row_x, row_seg, x_local, segments, gx_count, gz_count, after
):
    rows, tests = misfit.shape
    m = 2 * gx_count * gz_count
    cell = (row_seg * x_local + row_x).reshape(rows, 1)
    return pl.pallas_call(
        functools.partial(prepare_kernel, gz_count),
        in_specs=[SMEM, VMEM, VMEM, VMEM, ANY],
        out_specs=[VMEM] * (1 + len(CHUNKS)),
        out_shape=[jax.ShapeDtypeStruct((rows, x_local * segments), jnp.bfloat16)]
        + [jax.ShapeDtypeStruct((size, 2 * m, 2 * rows), jnp.bfloat16) for size in CHUNKS],
        compiler_params=params(24),
        cost_estimate=cost(0, 6 * MIB),
        name="prepare",
    )(row_count, misfit.T.reshape(tests // 2, 2 * rows), row_owner.T, cell, after)


def x_kernel(first, waits, resident, ends, own, above, below, leak, inverse, *rest):
    out, own_v, above_v, below_v, leak_v, inverse_v, vertical, staged, sems, block_sems, out_sems = rest[
        waits:
    ]
    tests, _, lines, _ = own_v.shape
    cells = staged.shape[0]
    size = cells // BLOCKS
    leak_copy = fetch(leak, leak_v, sems.at[3 * tests])
    parts = [
        [
            fetch(own.at[pl.ds(first + t, 1)], own_v.at[pl.ds(t, 1)], sems.at[3 * t]),
            fetch(above.at[pl.ds(t, 1)], above_v.at[pl.ds(t, 1)], sems.at[3 * t + 1]),
            fetch(below.at[pl.ds(t, 1)], below_v.at[pl.ds(t, 1)], sems.at[3 * t + 2]),
        ]
        for t in range(tests)
    ]
    blocks = []

    def fetch_blocks(upto):
        for k in range(len(blocks), 0 if resident else min(upto, BLOCKS)):
            part = pl.ds(k * size, size)
            blocks.append(fetch(inverse.at[:, part], inverse_v.at[:, part], block_sems.at[k]))

    leak_copy.wait()
    for t in range(tests):
        for copy in parts[t]:
            copy.wait()
        fetch_blocks((t + 1) * BLOCKS // tests)
        centre = own_v[t, 0].astype(jnp.float32)
        near = above_v[t, 0].astype(jnp.float32) * ends[0] + below_v[t, 0].astype(jnp.float32) * ends[1]
        vertical[t * lines : (t + 1) * lines] = (
            centre + leak_v[0] * (near - 2.0 * centre)
        ).astype(jnp.bfloat16)
    fetch_blocks(BLOCKS)
    sent = []
    matrix = inverse if resident else inverse_v
    for k in range(BLOCKS):
        if not resident:
            blocks[k].wait()
        part = matrix[0, k * size : (k + 1) * size]
        if resident:
            staged[k * size : (k + 1) * size] = lax.dot_general(
                part, vertical[...], NT, preferred_element_type=jnp.float32
            ).astype(jnp.bfloat16)
        else:
            staged[k * size : (k + 1) * size] = (
                lax.dot_general(vertical[...], part, NT, preferred_element_type=jnp.float32)
                .astype(jnp.bfloat16)
                .T
            )
        sent.append(
            fetch(staged.at[pl.ds(k * size, size)], out.at[pl.ds(k * size, size)], out_sems.at[k])
        )
    for copy in sent:
        copy.wait()


def x_sweep(own, first, above, below, leak, inverse, ends, after, resident):
    tests, _, lines, width = above.shape
    cells = inverse.shape[1]
    part = pltpu.VMEM(above.shape, above.dtype)
    return pl.pallas_call(
        functools.partial(x_kernel, first, len(after), resident),
        in_specs=[SMEM, HBM, ANY, ANY, HBM, VMEM if resident else HBM] + [ANY] * len(after),
        out_specs=HBM,
        out_shape=pltpu.HBM((cells, tests * lines), jnp.bfloat16),
        scratch_shapes=[
            part,
            part,
            part,
            pltpu.VMEM(leak.shape, leak.dtype),
            pltpu.VMEM((1, 8, 128) if resident else inverse.shape, inverse.dtype),
            pltpu.VMEM((tests * lines, width), jnp.bfloat16),
            pltpu.VMEM((cells, tests * lines), jnp.bfloat16),
            pltpu.SemaphoreType.DMA((3 * tests + 1,)),
            pltpu.SemaphoreType.DMA((BLOCKS,)),
            pltpu.SemaphoreType.DMA((BLOCKS,)),
        ],
        compiler_params=params(RESIDENT_LIMIT if resident else X_LIMIT),
        cost_estimate=cost(2 * cells * tests * lines * width, 20 * MIB),
        name="x_sweep",
    )(ends, own, above, below, leak, inverse, *after)


def y_kernel(first, earlier, swept, inverse, hot, weights, *rest):
    befores = rest[:earlier]
    out, partial, swept_v, inverse_v, hot_v, weights_v, lines, staged, picked, sems, block_sems, out_sems = rest[-12:]
    inputs = [
        fetch(source, buffer, sems.at[i])
        for i, (source, buffer) in enumerate(
            [(swept, swept_v), (hot, hot_v), (weights, weights_v)]
        )
    ]
    sources, x_local, lanes = swept_v.shape
    pairs = lanes // SEG
    tests = 2 * pairs
    y_local = SEG // 2
    cells = inverse_v.shape[1]
    blocks = [
        fetch(
            inverse.at[:, pl.ds(k, BLOCK)], inverse_v.at[:, pl.ds(k, BLOCK)], block_sems.at[k // BLOCK]
        )
        for k in range(0, cells, BLOCK)
    ]

    group = weights_v.shape[1] // 2 // sources
    place = 0
    for i, before in enumerate(befores):
        inputs.append(
            fetch(before, partial.at[:, pl.ds(place, before.shape[1])], sems.at[3 + i])
        )
        place += before.shape[1]

    inputs[0].wait()
    for p in range(pairs):
        for s in range(sources // 2):
            a = swept_v[2 * s, :, p * SEG : (p + 1) * SEG]
            b = swept_v[2 * s + 1, :, p * SEG : (p + 1) * SEG]
            for t in range(2):
                cut = slice(t * y_local, (t + 1) * y_local)
                lines[
                    (2 * p + t) * x_local : (2 * p + t + 1) * x_local,
                    s * SEG : (s + 1) * SEG,
                ] = jnp.concatenate([a[:, cut], b[:, cut]], axis=1)

    sent = []
    for k in range(0, cells, BLOCK):
        blocks[k // BLOCK].wait()
        done = lax.dot_general(
            lines[...], inverse_v[0, k : k + BLOCK], NT, preferred_element_type=jnp.float32
        ).astype(jnp.bfloat16)
        for t in range(tests):
            staged[t, 0, :, k : k + BLOCK] = done[t * x_local : (t + 1) * x_local]
        sent.append(
            fetch(
                staged.at[:, :, :, pl.ds(k, BLOCK)],
                out.at[pl.ds(first, tests), :, :, pl.ds(k, BLOCK)],
                out_sems.at[k // BLOCK],
            )
        )
        if k == 0:
            inputs[1].wait()
        first_cell = k // SEG * x_local
        for p in range(pairs):
            stack = []
            for s in range(0, BLOCK, SEG):
                stack.append(
                    jnp.concatenate(
                        [
                            done[(2 * p + t) * x_local : (2 * p + t + 1) * x_local, s : s + SEG]
                            for t in range(2)
                        ],
                        axis=1,
                    )
                )
            stack = jnp.concatenate(stack, axis=0)
            found = jnp.dot(
                hot_v[:, first_cell : first_cell + stack.shape[0]],
                stack,
                preferred_element_type=jnp.float32,
            )
            if k == 0:
                picked[p] = found
            else:
                picked[p] += found

    inputs[2].wait()
    for p in range(pairs):
        rows = picked[p].astype(jnp.bfloat16)
        both = jnp.dot(
            weights_v[p],
            jnp.concatenate([rows[:, :SEG], rows[:, SEG:]], axis=0),
            preferred_element_type=jnp.float32,
        )
        half = both.shape[0] // 2
        partial[:, place + p * group : place + (p + 1) * group] = (
            (both[:half] + both[half:])
            .reshape(partial.shape[0], group, SEG)
            .astype(jnp.bfloat16)
        )
    for copy in inputs[3:] + sent:
        copy.wait()


def y_sweep(swept, inverse, hot, weights, adjoint, befores, first, tests_total, limit):
    sources, x_local, lanes = swept.shape
    pairs = lanes // SEG
    tests = 2 * pairs
    cells = inverse.shape[1]
    rows = hot.shape[0]
    group = weights.shape[1] // 2 // sources
    height = pairs * group + sum(before.shape[1] for before in befores)
    operands = [swept, inverse, hot, weights, *befores]
    in_specs = [ANY] + [HBM] * 3 + [ANY] * len(befores)
    aliases = {}
    if adjoint is not None:
        aliases = {len(operands): 0}
        operands.append(adjoint)
        in_specs.append(ANY)
    return pl.pallas_call(
        functools.partial(y_kernel, first, len(befores)),
        in_specs=in_specs,
        out_specs=[ANY, VMEM],
        out_shape=[
            jax.ShapeDtypeStruct((tests_total, 1, x_local, cells), jnp.bfloat16),
            jax.ShapeDtypeStruct((sources, height, SEG), jnp.bfloat16),
        ],
        scratch_shapes=[
            pltpu.VMEM(swept.shape, swept.dtype),
            pltpu.VMEM(inverse.shape, inverse.dtype),
            pltpu.VMEM(hot.shape, hot.dtype),
            pltpu.VMEM(weights.shape, weights.dtype),
            pltpu.VMEM((tests * x_local, cells), jnp.bfloat16),
            pltpu.VMEM((tests, 1, x_local, cells), jnp.bfloat16),
            pltpu.VMEM((pairs, rows, 2 * SEG), jnp.float32),
            pltpu.SemaphoreType.DMA((3 + len(befores),)),
            pltpu.SemaphoreType.DMA((cells // BLOCK,)),
            pltpu.SemaphoreType.DMA((cells // BLOCK,)),
        ],
        input_output_aliases=aliases,
        compiler_params=params(limit),
        cost_estimate=cost(2 * cells * tests * x_local * cells, 20 * MIB),
        name="y_sweep",
    )(*operands)


def body(heads, leak, x_inverse, y_inverse, misfit, row_owner, row_count, row_x, row_seg):
    tests, _, y_local, nx = heads.shape
    gx_count = lax.axis_size("gx")
    gz_count = lax.axis_size("gz")
    x_local = nx // gx_count
    ny = y_inverse.shape[1]
    up = [(i, (i + 1) % gz_count) for i in range(gz_count)]
    down = [((i + 1) % gz_count, i) for i in range(gz_count)]
    layer = lax.axis_index("gz")
    ends = jnp.stack([layer < gz_count - 1, layer > 0]).astype(jnp.float32)

    spans = [(2 * sum(CHUNKS[:c]), 2 * size) for c, size in enumerate(CHUNKS)]
    parts = [split(heads, *spans[0], space=pltpu.VMEM)]
    hot, *weights = prepare(
        misfit,
        row_owner,
        row_count,
        row_x,
        row_seg,
        x_local,
        ny // SEG,
        gx_count,
        gz_count,
        parts[0],
    )
    later = [split(heads, *span, after=[hot]) for span in spans[2:]]
    parts += [split(heads, *spans[1], after=[hot]), *later]
    below = [lax.ppermute(p, "gz", up) for p in parts]
    arrived = [(lax.ppermute(p, "gz", down), b) for p, b in zip(parts, below)]
    adjoint = None
    order = [[hot, *parts[2:]], [], []]
    partials = []
    for c, (first, size) in enumerate(spans):
        resident = c < RESIDENT
        matrix = load(x_inverse, parts[c + 1]) if resident else x_inverse
        own, place = (parts[c], 0) if resident else (heads, first)
        lines = x_sweep(own, place, *arrived[c], leak, matrix, ends, order[c], resident)
        swept = lines.reshape(gx_count, x_local, size * y_local)
        swept = lax.all_to_all(swept, "gx", split_axis=0, concat_axis=0, tiled=True)
        befores = partials if c == len(spans) - 1 else []
        adjoint, partial = y_sweep(
            swept,
            y_inverse,
            hot,
            weights[c],
            adjoint,
            befores,
            first,
            tests,
            LAST_LIMIT if befores else Y_LIMIT,
        )
        partials.append(partial)
        order.append([partial])

    sent = partials[-1].reshape(gx_count, tests, gz_count, SEG)
    sent = jnp.transpose(sent, (0, 2, 1, 3)).reshape(gx_count * gz_count, tests, SEG)
    got = lax.all_to_all(sent, ("gx", "gz"), split_axis=0, concat_axis=0, tiled=True)
    return (adjoint, jnp.sum(got.astype(jnp.float32), axis=0)[None])


def solution(mesh):
    placed = (
        P(None, "gz", "gx", None),
        P("gz", "gx", None),
        P("gz", None, None),
        P("gz", None, None),
        P(("gx", "gz"), None),
        P(("gx", "gz"), None),
        P(("gx", "gz")),
        P(("gx", "gz")),
        P(("gx", "gz")),
    )
    return jax.shard_map(
        body,
        mesh=mesh,
        in_specs=placed,
        out_specs=(P(None, "gz", "gx", None), P(("gx", "gz"), None, None)),
        check_vma=False,
    )
```
